512 devices in a mesh: pipe: 32 (over y, z_hi), dp: 16 (over x, z_lo, core).
Axes of the slice: x: 4, y: 8, z: 8 (z_hi: 4, z_lo: 2; z = z_hi * 2 + z_lo), core: 2. Of those that a mesh axis runs over, the one named last changes fastest.
Arguments:
- corrected: bfloat16 [32, 2176, 6144], P('pipe', 'dp'), may hold values from -6 to 6
- inputs: bfloat16 [32, 2176, 6144], P('pipe', 'dp'), may hold values from -0.09375 to 0.09375
- act_basis: bfloat16 [32, 6144, 64], P('pipe', 'dp'), may hold values from -0.078125 to 0.078125
- weight_basis: bfloat16 [32, 6144, 64], P('pipe', 'dp'), may hold values from -0.078125 to 0.078125
Outputs:
- new_error: bfloat16 [32, 2176, 6144], P('pipe', 'dp')
- weight_right: float32 [32, 6144, 64], P('pipe', 'dp')
The draws below stay inside these ranges and needn't reach their ends.
All inputs are finite; a program needn't handle non-finite values.
Results may differ from the reference program's by a relative error of at most 0.025.
Values may be sent and summed in bfloat16 or wider, within the bound.
No kernel may reach another device: no remote copies, remote signals or barrier semaphores. Data moves between devices by JAX's collectives and lax.ppermute only.
A program may use at most 64 MiB of HBM per device.

```python
import jax
import jax.numpy as jnp
from jax import lax

D = 6144
RANK = 64
ROWS = 136
SECTIONS = 32
TOKENS = 2176
N_PIPE = 32
N_DP = 16


def shard_levels(stream_key, extent, split, least, high):
    level, own = 1.0, jax.random.fold_in(stream_key, 6)
    for dim, blocks in split:
        heights = jnp.exp(jax.random.uniform(jax.random.fold_in(own, dim), (blocks,), jnp.float32, least / len(split), high / len(split)))
        level = level * jnp.repeat(heights, extent[dim] // blocks).reshape([-1 if axis == dim else 1 for axis in range(len(extent))])
    return level


def noise(rng, extent, width, most, cuts=(), held_as=jnp.bfloat16):
    values = jax.random.normal(rng, extent, jnp.float32) * width
    if len(cuts) > 0:
        values = shard_levels(rng, extent, cuts, -0.22, 0.18) * values
    return jnp.clip(values, min=-most, max=most).astype(held_as)


def setup_inputs(seed: int = 0) -> dict:
    key_of = jax.random.split(jax.random.key(seed), 5)
    return {
        "corrected": noise(key_of[0], (SECTIONS, TOKENS, D), 1.0, 6.0, ((0, 32), (1, 16))),
        "inputs": noise(key_of[1], (SECTIONS, TOKENS, D), 0.015625, 0.09375, ((0, 32), (1, 16))),
        "act_basis": noise(key_of[2], (SECTIONS, D, RANK), D ** -0.5, 0.078125, ((0, 32), (1, 16))),
        "weight_basis": noise(key_of[3], (SECTIONS, D, RANK), D ** -0.5, 0.078125, ((0, 32), (1, 16))),
    }


HIGH = lax.Precision.HIGHEST

def orthonormal(matrix):
    gram_mat = jnp.dot(matrix.T, matrix, precision=HIGH)
    cholesky_low = jnp.linalg.cholesky(gram_mat)
    return jax.scipy.linalg.solve_triangular(cholesky_low, matrix.T, lower=True).T

def compress_one(micro_rows, basis):
    left_raw = jnp.dot(micro_rows.astype(jnp.float32), basis.astype(jnp.float32), preferred_element_type=jnp.float32)
    left_unit = orthonormal(left_raw).astype(jnp.bfloat16)
    right_factor = jnp.dot(micro_rows.T.astype(jnp.float32), left_unit.astype(jnp.float32), preferred_element_type=jnp.float32).astype(jnp.bfloat16)
    approx = jnp.dot(left_unit.astype(jnp.float32), right_factor.T.astype(jnp.float32), preferred_element_type=jnp.float32)
    error_rows = (micro_rows.astype(jnp.float32) - approx).astype(jnp.bfloat16)
    return (left_unit, right_factor, error_rows)

def section_compress(operands):
    micro_all, basis = operands
    return jax.vmap(compress_one, in_axes=(0, None))(micro_all, basis)

def section_weight(operands):
    input_all, left_all, right_all, wbasis = operands

    def term_left(x_rows, left_in, right_in):
        inner = jnp.dot(right_in.T.astype(jnp.float32), wbasis.astype(jnp.float32), preferred_element_type=jnp.float32)
        coeff = jnp.dot(left_in.astype(jnp.float32), inner, precision=HIGH).astype(jnp.bfloat16)
        return jnp.dot(x_rows.T.astype(jnp.float32), coeff.astype(jnp.float32), preferred_element_type=jnp.float32)
    left_sum = jnp.sum(jax.vmap(term_left)(input_all, left_all, right_all), axis=0)
    unit_b = orthonormal(left_sum).astype(jnp.bfloat16)

    def term_right(x_rows, left_in, right_in):
        middle = jnp.dot(x_rows.astype(jnp.float32), unit_b.astype(jnp.float32), preferred_element_type=jnp.float32)
        small_b = jnp.dot(left_in.astype(jnp.float32).T, middle, precision=HIGH).astype(jnp.bfloat16)
        return jnp.dot(right_in.astype(jnp.float32), small_b.astype(jnp.float32), preferred_element_type=jnp.float32)
    return jnp.sum(jax.vmap(term_right)(input_all, left_all, right_all), axis=0)

def reference(corrected, inputs, act_basis, weight_basis):
    micro = corrected.reshape(N_PIPE, N_DP, ROWS, D)
    left_all, right_all, error_all = lax.map(section_compress, (micro, act_basis))
    left_recv = jnp.roll(left_all, -1, axis=0)
    right_recv = jnp.roll(right_all, -1, axis=0)
    input_rows = inputs.reshape(N_PIPE, N_DP, ROWS, D)
    weight_right = lax.map(section_weight, (input_rows, left_recv, right_recv, weight_basis))
    return (error_all.reshape(N_PIPE, N_DP * ROWS, D), weight_right)
```

```python
import jax
import jax.numpy as jnp
from jax import lax
from jax.experimental import pallas as pl
from jax.experimental.pallas import tpu as pltpu
from jax.sharding import PartitionSpec as P

HIGH = lax.Precision.HIGHEST
F32, BF16 = jnp.float32, jnp.bfloat16
D, RANK, ROWS, DP = 6144, 64, 136, 16
SLICE = D // DP
ACROSS = [[2 * i + c for i in range(8)] for c in range(2)]
NT = (((1,), (1,)), ((), ()))
TN = (((0,), (0,)), ((), ()))


def passed_along(shard, axis, by):
    devices = lax.axis_size(axis)
    return lax.ppermute(shard, axis, [(i, (i + by) % devices) for i in range(devices)])


def inverse_cholesky(gram):
    wide = jnp.concatenate([gram, jnp.eye(RANK, dtype=F32)], axis=1)
    sub = lax.broadcasted_iota(jnp.int32, (8, 128), 0)
    part = [wide[8 * g : 8 * g + 8] for g in range(8)]
    for k in range(0, RANK, 4):
        own, r = divmod(k, 8)
        rows = [part[own][r + i : r + i + 1, :] for i in range(4)]
        s = [[jnp.broadcast_to(rows[i][:, k + j : k + j + 1], (1, 128)) for j in range(4)] for i in range(4)]
        done, inv, low = list(rows), [None] * 4, {}
        for i in range(4):
            inv[i] = 1.0 / s[i][i]
            for t in range(i + 1, 4):
                low[t, i] = s[i][t] * inv[i]
                for j in range(t, 4):
                    s[t][j] = s[t][j] - low[t, i] * s[i][j]
                done[t] = done[t] - low[t, i] * done[i]
        solved = [done[i] * inv[i] for i in range(4)]
        for i in (2, 1, 0):
            for t in range(i + 1, 4):
                solved[i] = solved[i] - low[t, i] * solved[t]
        for g in range(own, 8):
            if g > own or r == 0:
                less = part[g] - sum(part[g][:, k + i : k + i + 1] * solved[i] for i in range(4))
            if g > own:
                part[g] = less
            else:
                part[g] = jnp.where(sub > r + 3, less, part[g]) if r == 0 else part[g]
                for i in range(1, 4):
                    part[g] = jnp.where(sub == r + i, done[i], part[g])
    wide = jnp.concatenate(part, axis=0)
    square = (RANK, RANK)
    on_diagonal = lax.broadcasted_iota(jnp.int32, square, 0) == lax.broadcasted_iota(jnp.int32, square, 1)
    pivots = jnp.sum(jnp.where(on_diagonal, wide[:, :RANK], 0.0), axis=1, keepdims=True)
    return wide[:, RANK:] * lax.rsqrt(pivots)


def half_product(micro_ref, half_ref, core):
    total = jnp.zeros((2 * RANK, ROWS), F32)
    for i in range(DP // 2):
        at = pl.ds(pl.multiple_of((2 * i + core) * SLICE, 128), SLICE)
        total += lax.dot_general(half_ref[i], micro_ref[:, at], NT, preferred_element_type=F32)
    return total


def own_half(core_ref, micro_ref, own_ref, out_ref):
    out_ref[...] = half_product(micro_ref, own_ref, core_ref[0])


def compress(core_ref, micro_ref, other_ref, part_ref, factors_ref, right_ref):
    total = part_ref[...] + half_product(micro_ref, other_ref, 1 - core_ref[0])
    raw, warm = total[:RANK], total[RANK:]
    gram = lax.dot_general(raw, raw, NT, precision=HIGH, preferred_element_type=F32)
    left = jnp.dot(inverse_cholesky(gram), raw, precision=HIGH, preferred_element_type=F32).astype(BF16)
    inner = lax.dot_general(left.astype(F32), warm, NT, precision=HIGH, preferred_element_type=F32)
    factors_ref[...] = jnp.zeros_like(factors_ref)
    factors_ref[:, :ROWS] = left
    factors_ref[:, 192:] = inner.astype(BF16)
    for j in range(DP):
        at = slice(j * SLICE, (j + 1) * SLICE)
        right_ref[:, at] = jnp.dot(left, micro_ref[:, at], preferred_element_type=F32).astype(BF16)


def residual(micro_ref, factors_ref, right_ref, error_ref):
    left = factors_ref[:, :ROWS]
    for j in range(DP):
        at = slice(j * SLICE, (j + 1) * SLICE)
        approx = lax.dot_general(left, right_ref[:, at], TN, preferred_element_type=F32)
        error_ref[:, at] = (micro_ref[:, at].astype(F32) - approx).astype(BF16)


def project(rows_ref, factors_ref, out_ref):
    left, inner = factors_ref[:, :ROWS], factors_ref[:, 192:]
    for j in range(DP):
        at = slice(j * SLICE, (j + 1) * SLICE)
        term = jnp.dot(left, rows_ref[:, at], preferred_element_type=F32).astype(BF16)
        for c in range(3):
            out_ref[j, c * RANK : (c + 1) * RANK, :] = term[:, c * 128 : (c + 1) * 128]
        out_ref[j, 3 * RANK :, :RANK] = inner[:32]
        out_ref[j, 3 * RANK :, RANK:] = inner[32:]


def accumulate(in_ref, out_ref):
    panels = [in_ref[:, c * RANK : (c + 1) * RANK, :].reshape(DP * RANK, 128) for c in range(3)]
    terms = jnp.concatenate(panels, axis=1)
    mixed = in_ref[:, 3 * RANK :, :].reshape(DP * 32, 128)
    inner = jnp.concatenate(
        [mixed[:, :RANK].reshape(DP, 32, RANK), mixed[:, RANK:].reshape(DP, 32, RANK)], axis=1
    ).reshape(DP * RANK, RANK)
    whole = lax.dot_general(inner, terms, TN, preferred_element_type=F32)
    gram = lax.dot_general(whole, whole, NT, precision=HIGH, preferred_element_type=F32)
    high = whole.astype(BF16)
    low = (whole - high.astype(F32)).astype(BF16)
    met = lax.dot_general(high, terms, NT, preferred_element_type=F32)
    met += lax.dot_general(low, terms, NT, preferred_element_type=F32)
    for r in range(DP):
        out_ref[r, :, :RANK] = met[:, r * RANK : (r + 1) * RANK]
        out_ref[r, :, RANK:] = gram


def add_sums(in_ref, out_ref):
    total = in_ref[0]
    for j in range(1, DP):
        total += in_ref[j]
    out_ref[...] = total


def factor(in_ref, out_ref):
    out_ref[...] = inverse_cholesky(in_ref[:, RANK:])


def expand(met_ref, right_ref, out_ref):
    small = met_ref[:, :RANK].astype(BF16)
    for j in range(DP):
        at = slice(j * SLICE, (j + 1) * SLICE)
        out_ref[j] = jnp.dot(small, right_ref[:, at], preferred_element_type=F32).astype(BF16)


def add_up(in_ref, out_ref):
    total = in_ref[0].astype(F32)
    for r in range(1, DP):
        total += in_ref[r].astype(F32)
    out_ref[...] = total


VMEM = pl.BlockSpec(memory_space=pltpu.VMEM)
SMEM = pl.BlockSpec(memory_space=pltpu.SMEM)


def finish(inverse_ref, in_ref, out_ref):
    out_ref[...] = jnp.dot(inverse_ref[...], in_ref[...], precision=HIGH, preferred_element_type=F32)


def kernel(body, *shapes, flops, specs=None):
    outs = [jax.ShapeDtypeStruct(shape, dtype) for shape, dtype in shapes]
    return pl.pallas_call(
        body,
        out_shape=outs if len(outs) > 1 else outs[0],
        in_specs=specs or [VMEM] * (body.__code__.co_argcount - len(outs)),
        compiler_params=pltpu.CompilerParams(vmem_limit_bytes=32 * 2**20),
        cost_estimate=pl.CostEstimate(flops=flops, bytes_accessed=4 * 2**20, transcendentals=0),
        name=body.__name__,
    )


def local(corrected, inputs, act_basis, weight_basis):
    micro, rows = corrected[0], inputs[0]
    warm = passed_along(weight_basis[0].T, "pipe", 1)
    both = jnp.concatenate([act_basis[0].T, warm], axis=0)
    both = lax.all_to_all(
        jnp.broadcast_to(both, (8, *both.shape)), "dp", 0, 0, tiled=True, axis_index_groups=ACROSS
    )
    core = (lax.axis_index("dp") % 2).reshape(1)
    other = lax.ppermute(both, "dp", [(i, i ^ 1) for i in range(DP)])
    product = 2 * ROWS * D * RANK
    part = kernel(own_half, ((2 * RANK, ROWS), F32), flops=product, specs=[SMEM, VMEM, VMEM])(core, micro, both)
    factors, right = kernel(
        compress, ((RANK, 256), BF16), ((RANK, D), BF16), flops=2 * product, specs=[SMEM, VMEM, VMEM, VMEM]
    )(core, micro, other, part)
    factors_in = passed_along(factors, "pipe", -1)
    error = kernel(residual, ((ROWS, D), BF16), flops=product)(micro, factors, right)
    terms = kernel(project, ((DP, 224, 128), BF16), flops=product)(rows, factors_in)
    terms = lax.all_to_all(terms, "dp", 0, 0, tiled=True)
    sums = kernel(accumulate, ((DP, RANK, 128), F32), flops=product)(terms)
    sums = lax.all_to_all(sums, "dp", 0, 0, tiled=True)
    total = kernel(add_sums, ((RANK, 128), F32), flops=0)(sums)
    met = passed_along(total, "pipe", 1)
    inverse = kernel(factor, ((RANK, RANK), F32), flops=4 * product)(total)
    parts = kernel(expand, ((DP, RANK, SLICE), BF16), flops=product)(met, right)
    parts = lax.all_to_all(parts, "dp", 0, 0, tiled=True)
    parts = passed_along(kernel(add_up, ((RANK, SLICE), F32), flops=product)(parts), "pipe", -1)
    weight_right = kernel(finish, ((RANK, SLICE), F32), flops=0)(inverse, parts)
    return error[None], weight_right.T[None]


def solution(mesh):
    spec = P("pipe", "dp", None)
    return jax.shard_map(local, mesh=mesh, in_specs=(spec,) * 4, out_specs=(spec, spec), check_vma=False)
```

```python
import jax
import jax.numpy as jnp
from jax import lax
from jax.experimental import pallas as pl
from jax.experimental.pallas import tpu as pltpu
from jax.sharding import PartitionSpec as P

HIGH = lax.Precision.HIGHEST
F32, BF16 = jnp.float32, jnp.bfloat16
D, RANK, ROWS, DP = 6144, 64, 136, 16
SLICE = D // DP
HALF = DP // 2
CORES = [[2 * i, 2 * i + 1] for i in range(HALF)]
ACROSS = [[2 * i + c for i in range(HALF)] for c in range(2)]
NT = (((1,), (1,)), ((), ()))
TN = (((0,), (0,)), ((), ()))


def passed_along(shard, by):
    devices = lax.axis_size("pipe")
    return lax.ppermute(shard, "pipe", [(i, (i + by) % devices) for i in range(devices)])


def exchanged(shard):
    return lax.ppermute(shard, "dp", [(i, i ^ 1) for i in range(DP)])


def both_cores(shard):
    return lax.all_gather(shard, "dp", axis_index_groups=CORES)


def across(blocks):
    return lax.all_to_all(blocks, "dp", 0, 0, tiled=True, axis_index_groups=ACROSS)


def strip(i, core):
    return pl.ds(pl.multiple_of((2 * i + core) * SLICE, 128), SLICE)


def inverse_cholesky(gram):
    wide = jnp.concatenate([gram, jnp.eye(RANK, dtype=F32)], axis=1)
    sub = lax.broadcasted_iota(jnp.int32, (8, 128), 0)
    part = [wide[8 * g : 8 * g + 8] for g in range(8)]
    for k in range(0, RANK, 4):
        own, r = divmod(k, 8)
        rows = [part[own][r + i : r + i + 1, :] for i in range(4)]
        s = [[jnp.broadcast_to(rows[i][:, k + j : k + j + 1], (1, 128)) for j in range(4)] for i in range(4)]
        done, inv, low = list(rows), [None] * 4, {}
        for i in range(4):
            inv[i] = 1.0 / s[i][i]
            for t in range(i + 1, 4):
                low[t, i] = s[i][t] * inv[i]
                for j in range(t, 4):
                    s[t][j] = s[t][j] - low[t, i] * s[i][j]
                done[t] = done[t] - low[t, i] * done[i]
        solved = [done[i] * inv[i] for i in range(4)]
        for i in (2, 1, 0):
            for t in range(i + 1, 4):
                solved[i] = solved[i] - low[t, i] * solved[t]
        for g in range(own, 8):
            if g > own or r == 0:
                less = part[g] - sum(part[g][:, k + i : k + i + 1] * solved[i] for i in range(4))
            if g > own:
                part[g] = less
            else:
                part[g] = jnp.where(sub > r + 3, less, part[g]) if r == 0 else part[g]
                for i in range(1, 4):
                    part[g] = jnp.where(sub == r + i, done[i], part[g])
    wide = jnp.concatenate(part, axis=0)
    square = (RANK, RANK)
    on_diagonal = lax.broadcasted_iota(jnp.int32, square, 0) == lax.broadcasted_iota(jnp.int32, square, 1)
    pivots = jnp.sum(jnp.where(on_diagonal, wide[:, :RANK], 0.0), axis=1, keepdims=True)
    return wide[:, RANK:] * lax.rsqrt(pivots)


def split_halves(core_ref, in_ref, own_ref, other_ref):
    core = core_ref[0]
    for i in range(HALF):
        own_ref[i] = in_ref[:, strip(i, core)]
        other_ref[i] = in_ref[:, strip(i, 1 - core)]


def copies(one_ref, two_ref, out_ref):
    for i in range(HALF):
        out_ref[i, :RANK, :] = one_ref[...]
        out_ref[i, RANK:, :] = two_ref[...]


def half_product(core_ref, own_ref, other_ref, both_ref, out_ref):
    core = core_ref[0]
    own, other = jnp.zeros((ROWS, 2 * RANK), F32), jnp.zeros((ROWS, 2 * RANK), F32)
    for i in range(HALF):
        own += lax.dot_general(own_ref[i], both_ref[i], NT, preferred_element_type=F32)
        other += lax.dot_general(other_ref[i], both_ref[i], NT, preferred_element_type=F32)
    out_ref[core] = own
    out_ref[1 - core] = other


def factors_of(parts_ref, out_ref):
    total = [(parts_ref[0, slot] + parts_ref[1, slot]).T for slot in range(2)]
    raw = [both[:RANK] for both in total]
    gram = [lax.dot_general(a, a, NT, precision=HIGH, preferred_element_type=F32) for a in raw]
    inverse = [inverse_cholesky(a) for a in gram]
    for slot in range(2):
        left = jnp.dot(inverse[slot], raw[slot], precision=HIGH, preferred_element_type=F32).astype(BF16)
        inner = lax.dot_general(
            left.astype(F32), total[slot][RANK:], NT, precision=HIGH, preferred_element_type=F32
        )
        out_ref[slot] = jnp.zeros((RANK, 256), BF16)
        out_ref[slot, :, :ROWS] = left
        out_ref[slot, :, 192:] = inner.astype(BF16)


def against(core_ref, own_ref, other_ref, factors_ref, out_ref):
    core = core_ref[0]
    own, other = factors_ref[core, :, :ROWS], factors_ref[1 - core, :, :ROWS]
    at, to = pl.multiple_of(core * RANK, RANK), pl.multiple_of((1 - core) * RANK, RANK)
    for i in range(HALF):
        out_ref[i, pl.ds(at, RANK), :] = jnp.dot(
            own, own_ref[i], preferred_element_type=F32
        ).astype(BF16)
        out_ref[i, pl.ds(to, RANK), :] = jnp.dot(other, other_ref[i], preferred_element_type=F32).astype(BF16)


def project(core_ref, own_ref, other_ref, factors_ref, out_ref, term_ref):
    against(core_ref, own_ref, other_ref, factors_ref, out_ref)
    inner = jnp.concatenate([factors_ref[0, :, 192:], factors_ref[1, :, 192:]], axis=0)
    for i in range(HALF):
        term_ref[i] = lax.dot_general(inner, out_ref[i], TN, preferred_element_type=F32).astype(BF16)


def residual(core_ref, micro_ref, factors_ref, error_ref):
    left = factors_ref[core_ref[0], :, :ROWS]
    upright = left.astype(F32).T.astype(BF16)
    for j in range(DP):
        micro = micro_ref[:, j * SLICE : (j + 1) * SLICE]
        right = jnp.dot(left, micro, preferred_element_type=F32).astype(BF16)
        approx = jnp.dot(upright, right, preferred_element_type=F32)
        error_ref[:, j * SLICE : (j + 1) * SLICE] = (micro.astype(F32) - approx).astype(BF16)


def add_up(in_ref, out_ref):
    total = in_ref[0].astype(F32)
    for i in range(1, HALF):
        total += in_ref[i].astype(F32)
    out_ref[...] = total


def add_and_copy(in_ref, out_ref):
    total = in_ref[0].astype(F32)
    for i in range(1, HALF):
        total += in_ref[i].astype(F32)
    for i in range(HALF):
        out_ref[i] = total.astype(BF16)


def meet(whole_ref, terms_ref, out_ref):
    met, gram = jnp.zeros((RANK, 2 * RANK), F32), jnp.zeros((RANK, RANK), F32)
    for i in range(HALF):
        met += lax.dot_general(whole_ref[i], terms_ref[i], NT, preferred_element_type=F32)
        gram += lax.dot_general(whole_ref[i], whole_ref[i], NT, preferred_element_type=F32)
    out_ref[:, : 2 * RANK] = met
    out_ref[:, 2 * RANK : 3 * RANK] = gram
    out_ref[:, 3 * RANK :] = jnp.zeros((RANK, RANK), F32)


def add_met(parts_ref, out_ref):
    out_ref[...] = parts_ref[0, :, : 2 * RANK] + parts_ref[1, :, : 2 * RANK]


def factor(parts_ref, out_ref):
    at = slice(2 * RANK, 3 * RANK)
    out_ref[...] = inverse_cholesky(parts_ref[0, :, at] + parts_ref[1, :, at])


def expand(met_ref, right_ref, out_ref):
    met = met_ref[...].astype(BF16)
    for i in range(HALF):
        out_ref[i] = jnp.dot(met, right_ref[i], preferred_element_type=F32).astype(BF16)


def finish(inverse_ref, in_ref, out_ref):
    out_ref[...] = jnp.dot(inverse_ref[...], in_ref[...], precision=HIGH, preferred_element_type=F32)


VMEM = pl.BlockSpec(memory_space=pltpu.VMEM)
SMEM = pl.BlockSpec(memory_space=pltpu.SMEM)


def kernel(body, *shapes, flops=0):
    outs = [jax.ShapeDtypeStruct(shape, dtype) for shape, dtype in shapes]
    names = body.__code__.co_varnames[: body.__code__.co_argcount - len(outs)]
    return pl.pallas_call(
        body,
        out_shape=outs if len(outs) > 1 else outs[0],
        in_specs=[SMEM if name == "core_ref" else VMEM for name in names],
        compiler_params=pltpu.CompilerParams(vmem_limit_bytes=32 * 2**20),
        cost_estimate=pl.CostEstimate(flops=flops, bytes_accessed=2**20, transcendentals=0),
        name=body.__name__,
    )


def local(corrected, inputs, act_basis, weight_basis):
    micro, rows = corrected[0], inputs[0]
    core = (lax.axis_index("dp") % 2).reshape(1)
    product = 2 * ROWS * D * RANK
    halves = ((HALF, ROWS, SLICE), BF16)
    stacked = ((HALF, 2 * RANK, SLICE), BF16)
    blocks = ((HALF, RANK, SLICE), BF16)

    warm = passed_along(weight_basis[0].T, 1)
    both = across(kernel(copies, stacked)(act_basis[0].T, warm))
    micro_own, micro_other = kernel(split_halves, halves, halves)(core, micro)
    micro_other = exchanged(micro_other)
    rows_own, rows_other = kernel(split_halves, halves, halves)(core, rows)
    rows_other = exchanged(rows_other)
    part = kernel(half_product, ((2, ROWS, 2 * RANK), F32), flops=2 * product)(core, micro_own, micro_other, both)
    factors = kernel(factors_of, ((2, RANK, 256), BF16), flops=4 * product)(both_cores(part))
    factors_in = passed_along(factors, -1)
    error = kernel(residual, ((ROWS, D), BF16), flops=2 * product)(core, micro, factors)
    factors_in, error = lax.optimization_barrier((factors_in, error))
    right = kernel(against, stacked, flops=product)(core, micro_own, micro_other, factors)
    terms, summed = kernel(project, stacked, blocks, flops=product)(core, rows_own, rows_other, factors_in)
    whole = across(kernel(add_and_copy, blocks)(across(summed)))
    met = both_cores(kernel(meet, ((RANK, 256), F32), flops=product)(whole, terms))
    met_in = passed_along(kernel(add_met, ((RANK, 2 * RANK), F32))(met), 1)
    parts = across(kernel(expand, blocks, flops=product)(met_in, right))
    parts = passed_along(kernel(add_up, ((RANK, SLICE), F32))(parts), -1)
    inverse = kernel(factor, ((RANK, RANK), F32), flops=4 * product)(met)
    weight_right = kernel(finish, ((RANK, SLICE), F32))(inverse, parts)
    return error[None], weight_right.T[None]


def solution(mesh):
    spec = P("pipe", "dp", None)
    return jax.shard_map(local, mesh=mesh, in_specs=(spec,) * 4, out_specs=(spec, spec), check_vma=False)
```

```python
import jax
import jax.numpy as jnp
from jax import lax
from jax.experimental import pallas as pl
from jax.experimental.pallas import tpu as pltpu
from jax.sharding import PartitionSpec as P

HIGH = lax.Precision.HIGHEST
F32, BF16 = jnp.float32, jnp.bfloat16
D, RANK, ROWS, DP = 6144, 64, 136, 16
SLICE = D // DP
HALF = DP // 2
CORES = [[2 * i, 2 * i + 1] for i in range(HALF)]
ACROSS = [[2 * i + c for i in range(HALF)] for c in range(2)]
NT = (((1,), (1,)), ((), ()))
TN = (((0,), (0,)), ((), ()))


def passed_along(shard, by):
    devices = lax.axis_size("pipe")
    return lax.ppermute(shard, "pipe", [(i, (i + by) % devices) for i in range(devices)])


def exchanged(shard):
    return lax.ppermute(shard, "dp", [(i, i ^ 1) for i in range(DP)])


def both_cores(shard):
    return lax.all_gather(shard, "dp", axis_index_groups=CORES)


def across(blocks):
    return lax.all_to_all(blocks, "dp", 0, 0, tiled=True, axis_index_groups=ACROSS)


def strip(i, core):
    return pl.ds(pl.multiple_of((2 * i + core) * SLICE, 128), SLICE)


def inverse_cholesky(gram):
    wide = jnp.concatenate([gram, jnp.eye(RANK, dtype=F32)], axis=1)
    sub = lax.broadcasted_iota(jnp.int32, (8, 128), 0)
    part = [wide[8 * g : 8 * g + 8] for g in range(8)]
    for k in range(0, RANK, 4):
        own, r = divmod(k, 8)
        rows = [part[own][r + i : r + i + 1, :] for i in range(4)]
        s = {(i, j): jnp.broadcast_to(rows[i][:, k + j : k + j + 1], (1, 128)) for i in range(4) for j in range(i, 4)}
        a, b, c = s[0, 0], s[0, 1], s[1, 1]
        first = 1.0 / (a * c - b * b)
        e = [[(c * s[0, t] - b * s[1, t]) * first, (a * s[1, t] - b * s[0, t]) * first] for t in (2, 3)]
        d = s[2, 2] - s[0, 2] * e[0][0] - s[1, 2] * e[0][1]
        f = s[2, 3] - s[0, 2] * e[1][0] - s[1, 2] * e[1][1]
        h = s[3, 3] - s[0, 3] * e[1][0] - s[1, 3] * e[1][1]
        second = 1.0 / (d * h - f * f)
        y = [rows[2 + t] - e[t][0] * rows[0] - e[t][1] * rows[1] for t in (0, 1)]
        v = [(h * y[0] - f * y[1]) * second, (d * y[1] - f * y[0]) * second]
        z = [(c * rows[0] - b * rows[1]) * first, (a * rows[1] - b * rows[0]) * first]
        solved = [z[t] - e[0][t] * v[0] - e[1][t] * v[1] for t in (0, 1)] + v
        done = [rows[0], rows[1] - (b / a) * rows[0], y[0], y[1] - (f / d) * y[0]]
        for g in range(own, 8):
            if g > own or r == 0:
                less = part[g] - sum(part[g][:, k + i : k + i + 1] * solved[i] for i in range(4))
            if g > own:
                part[g] = less
            else:
                part[g] = jnp.where(sub > r + 3, less, part[g]) if r == 0 else part[g]
                for i in range(1, 4):
                    part[g] = jnp.where(sub == r + i, done[i], part[g])
    wide = jnp.concatenate(part, axis=0)
    square = (RANK, RANK)
    on_diagonal = lax.broadcasted_iota(jnp.int32, square, 0) == lax.broadcasted_iota(jnp.int32, square, 1)
    pivots = jnp.sum(jnp.where(on_diagonal, wide[:, :RANK], 0.0), axis=1, keepdims=True)
    return wide[:, RANK:] * lax.rsqrt(pivots)


def split_halves(core_ref, in_ref, own_ref, other_ref):
    core = core_ref[0]
    for i in range(HALF):
        own_ref[i] = in_ref[:, strip(i, core)]
        other_ref[i] = in_ref[:, strip(i, 1 - core)]


def copies(one_ref, two_ref, out_ref):
    for i in range(HALF):
        out_ref[i, :RANK, :] = one_ref[...]
        out_ref[i, RANK:, :] = two_ref[...]


def side_by_side(in_ref):
    return jnp.concatenate([in_ref[i] for i in range(HALF)], axis=1)


def half_product(core_ref, own_ref, other_ref, both_ref, out_ref):
    core, both = core_ref[0], side_by_side(both_ref)
    out_ref[core] = lax.dot_general(side_by_side(own_ref), both, NT, preferred_element_type=F32)
    out_ref[1 - core] = lax.dot_general(side_by_side(other_ref), both, NT, preferred_element_type=F32)


def factors_of(parts_ref, out_ref):
    total = [(parts_ref[0, slot] + parts_ref[1, slot]).T for slot in range(2)]
    raw = [both[:RANK] for both in total]
    gram = [lax.dot_general(a, a, NT, precision=HIGH, preferred_element_type=F32) for a in raw]
    inverse = [inverse_cholesky(a) for a in gram]
    for slot in range(2):
        left = jnp.dot(inverse[slot], raw[slot], precision=HIGH, preferred_element_type=F32).astype(BF16)
        inner = lax.dot_general(
            left.astype(F32), total[slot][RANK:], NT, precision=HIGH, preferred_element_type=F32
        )
        out_ref[slot] = jnp.zeros((RANK, 256), BF16)
        out_ref[slot, :, :ROWS] = left
        out_ref[slot, :, 192:] = inner.astype(BF16)


def against(core_ref, own_ref, other_ref, factors_ref, out_ref):
    core = core_ref[0]
    own, other = factors_ref[core, :, :ROWS], factors_ref[1 - core, :, :ROWS]
    at, to = pl.multiple_of(core * RANK, RANK), pl.multiple_of((1 - core) * RANK, RANK)
    for i in range(HALF):
        out_ref[i, pl.ds(at, RANK), :] = jnp.dot(
            own, own_ref[i], preferred_element_type=F32
        ).astype(BF16)
        out_ref[i, pl.ds(to, RANK), :] = jnp.dot(other, other_ref[i], preferred_element_type=F32).astype(BF16)


def project(core_ref, own_ref, other_ref, factors_ref, out_ref, term_ref):
    against(core_ref, own_ref, other_ref, factors_ref, out_ref)
    inner = jnp.concatenate([factors_ref[0, :, 192:], factors_ref[1, :, 192:]], axis=0)
    for i in range(HALF):
        term_ref[i] = lax.dot_general(inner, out_ref[i], TN, preferred_element_type=F32).astype(BF16)


def residual(core_ref, micro_ref, factors_ref, error_ref, right_ref):
    left = factors_ref[core_ref[0], :, :ROWS]
    upright = left.astype(F32).T.astype(BF16)
    strips = [slice(j * SLICE, (j + 1) * SLICE) for j in range(DP)]
    for at in strips:
        right_ref[:, at] = jnp.dot(left, micro_ref[:, at], preferred_element_type=F32).astype(BF16)
    for at in strips:
        approx = jnp.dot(upright, right_ref[:, at], preferred_element_type=F32)
        error_ref[:, at] = (micro_ref[:, at].astype(F32) - approx).astype(BF16)


def add_up(in_ref, out_ref):
    total = in_ref[0].astype(F32)
    for i in range(1, HALF):
        total += in_ref[i].astype(F32)
    out_ref[...] = total.astype(BF16)


def add_and_copy(in_ref, out_ref):
    total = in_ref[0].astype(F32)
    for i in range(1, HALF):
        total += in_ref[i].astype(F32)
    for i in range(HALF):
        out_ref[i] = total.astype(BF16)


def meet(whole_ref, terms_ref, out_ref):
    met, gram = jnp.zeros((RANK, 2 * RANK), F32), jnp.zeros((RANK, RANK), F32)
    for i in range(HALF):
        met += lax.dot_general(whole_ref[i], terms_ref[i], NT, preferred_element_type=F32)
        gram += lax.dot_general(whole_ref[i], whole_ref[i], NT, preferred_element_type=F32)
    out_ref[:, : 2 * RANK] = met
    out_ref[:, 2 * RANK : 3 * RANK] = gram
    out_ref[:, 3 * RANK :] = jnp.zeros((RANK, RANK), F32)


def add_met(parts_ref, out_ref):
    out_ref[...] = (parts_ref[0, :, : 2 * RANK] + parts_ref[1, :, : 2 * RANK]).astype(BF16)


def factor(parts_ref, out_ref):
    at = slice(2 * RANK, 3 * RANK)
    out_ref[...] = inverse_cholesky(parts_ref[0, :, at] + parts_ref[1, :, at])


def expand(met_ref, right_ref, out_ref):
    met = met_ref[...]
    for i in range(HALF):
        out_ref[i] = jnp.dot(met, right_ref[i], preferred_element_type=F32).astype(BF16)


def finish(inverse_ref, in_ref, out_ref):
    out_ref[...] = jnp.dot(inverse_ref[...], in_ref[...].astype(F32), precision=HIGH, preferred_element_type=F32)


VMEM = pl.BlockSpec(memory_space=pltpu.VMEM)
SMEM = pl.BlockSpec(memory_space=pltpu.SMEM)


def kernel(body, *shapes, flops=0, scratch=()):
    outs = [jax.ShapeDtypeStruct(shape, dtype) for shape, dtype in shapes]
    names = body.__code__.co_varnames[: body.__code__.co_argcount - len(outs) - len(scratch)]
    return pl.pallas_call(
        body,
        out_shape=outs if len(outs) > 1 else outs[0],
        in_specs=[SMEM if name == "core_ref" else VMEM for name in names],
        compiler_params=pltpu.CompilerParams(vmem_limit_bytes=10 * 2**20),
        cost_estimate=pl.CostEstimate(flops=flops, bytes_accessed=2**20, transcendentals=0),
        scratch_shapes=list(scratch),
        name=body.__name__,
    )


def local(corrected, inputs, act_basis, weight_basis):
    micro, rows = corrected[0], inputs[0]
    core = (lax.axis_index("dp") % 2).reshape(1)
    product = 2 * ROWS * D * RANK
    halves = ((HALF, ROWS, SLICE), BF16)
    stacked = ((HALF, 2 * RANK, SLICE), BF16)
    blocks = ((HALF, RANK, SLICE), BF16)

    warm = passed_along(weight_basis[0].T, 1)
    both = across(kernel(copies, stacked)(act_basis[0].T, warm))
    micro_own, micro_other = kernel(split_halves, halves, halves)(core, micro)
    micro_other = exchanged(micro_other)
    rows_own, rows_other = kernel(split_halves, halves, halves)(core, rows)
    rows_other = exchanged(rows_other)
    part = kernel(half_product, ((2, ROWS, 2 * RANK), F32), flops=2 * product)(core, micro_own, micro_other, both)
    factors = kernel(factors_of, ((2, RANK, 256), BF16), flops=4 * product)(both_cores(part))
    factors_in = passed_along(factors, -1)
    error = kernel(residual, ((ROWS, D), BF16), flops=2 * product, scratch=[pltpu.VMEM((RANK, D), BF16)])(core, micro, factors)
    factors_in, error = lax.optimization_barrier((factors_in, error))
    right = kernel(against, stacked, flops=product)(core, micro_own, micro_other, factors)
    terms, summed = kernel(project, stacked, blocks, flops=product)(core, rows_own, rows_other, factors_in)
    whole = across(kernel(add_and_copy, blocks)(across(summed)))
    met = both_cores(kernel(meet, ((RANK, 256), F32), flops=product)(whole, terms))
    met_in = passed_along(kernel(add_met, ((RANK, 2 * RANK), BF16))(met), 1)
    parts = across(kernel(expand, blocks, flops=product)(met_in, right))
    parts = passed_along(kernel(add_up, ((RANK, SLICE), BF16))(parts), -1)
    inverse = kernel(factor, ((RANK, RANK), F32), flops=4 * product)(met)
    weight_right = kernel(finish, ((RANK, SLICE), F32))(inverse, parts)
    return error[None], weight_right.T[None]


def solution(mesh):
    spec = P("pipe", "dp", None)
    return jax.shard_map(local, mesh=mesh, in_specs=(spec,) * 4, out_specs=(spec, spec), check_vma=False)
```

```python
import jax
import jax.numpy as jnp
from jax import lax
from jax.experimental import pallas as pl
from jax.experimental.pallas import tpu as pltpu
from jax.sharding import PartitionSpec as P

HIGH = lax.Precision.HIGHEST
F32, BF16 = jnp.float32, jnp.bfloat16
D, RANK, ROWS, DP = 6144, 64, 136, 16
SLICE = D // DP
HALF = DP // 2
CORES = [[2 * i, 2 * i + 1] for i in range(HALF)]
ACROSS = [[2 * i + c for i in range(HALF)] for c in range(2)]
NT = (((1,), (1,)), ((), ()))
TN = (((0,), (0,)), ((), ()))


def passed_along(shard, by):
    devices = lax.axis_size("pipe")
    return lax.ppermute(shard, "pipe", [(i, (i + by) % devices) for i in range(devices)])


def exchanged(shard):
    return lax.ppermute(shard, "dp", [(i, i ^ 1) for i in range(DP)])


def both_cores(shard):
    return lax.all_gather(shard, "dp", axis_index_groups=CORES)


def across(blocks):
    return lax.all_to_all(blocks, "dp", 0, 0, tiled=True, axis_index_groups=ACROSS)


def strip(i, core):
    return pl.ds(pl.multiple_of((2 * i + core) * SLICE, 128), SLICE)


def inverse_cholesky(gram):
    wide = jnp.concatenate([gram, jnp.eye(RANK, dtype=F32)], axis=1)
    sub = lax.broadcasted_iota(jnp.int32, (8, 128), 0)
    part = [wide[8 * g : 8 * g + 8] for g in range(8)]
    for k in range(0, RANK, 4):
        own, r = divmod(k, 8)
        rows = [part[own][r + i : r + i + 1, :] for i in range(4)]
        s = {(i, j): jnp.broadcast_to(rows[i][:, k + j : k + j + 1], (1, 128)) for i in range(4) for j in range(i, 4)}
        a, b, c = s[0, 0], s[0, 1], s[1, 1]
        first = 1.0 / (a * c - b * b)
        e = [[(c * s[0, t] - b * s[1, t]) * first, (a * s[1, t] - b * s[0, t]) * first] for t in (2, 3)]
        d = s[2, 2] - s[0, 2] * e[0][0] - s[1, 2] * e[0][1]
        f = s[2, 3] - s[0, 2] * e[1][0] - s[1, 2] * e[1][1]
        h = s[3, 3] - s[0, 3] * e[1][0] - s[1, 3] * e[1][1]
        second = 1.0 / (d * h - f * f)
        y = [rows[2 + t] - e[t][0] * rows[0] - e[t][1] * rows[1] for t in (0, 1)]
        v = [(h * y[0] - f * y[1]) * second, (d * y[1] - f * y[0]) * second]
        z = [(c * rows[0] - b * rows[1]) * first, (a * rows[1] - b * rows[0]) * first]
        solved = [z[t] - e[0][t] * v[0] - e[1][t] * v[1] for t in (0, 1)] + v
        done = [rows[0], rows[1] - (b / a) * rows[0], y[0], y[1] - (f / d) * y[0]]
        for g in range(own, 8):
            if g > own or r == 0:
                less = part[g] - sum(part[g][:, k + i : k + i + 1] * solved[i] for i in range(4))
            if g > own:
                part[g] = less
            else:
                part[g] = jnp.where(sub > r + 3, less, part[g]) if r == 0 else part[g]
                for i in range(1, 4):
                    part[g] = jnp.where(sub == r + i, done[i], part[g])
    wide = jnp.concatenate(part, axis=0)
    square = (RANK, RANK)
    on_diagonal = lax.broadcasted_iota(jnp.int32, square, 0) == lax.broadcasted_iota(jnp.int32, square, 1)
    pivots = jnp.sum(jnp.where(on_diagonal, wide[:, :RANK], 0.0), axis=1, keepdims=True)
    return wide[:, RANK:] * lax.rsqrt(pivots)


def split_halves(core_ref, in_ref, own_ref, other_ref):
    core = core_ref[0]
    for i in range(HALF):
        own_ref[i] = in_ref[:, strip(i, core)]
        other_ref[i] = in_ref[:, strip(i, 1 - core)]


def copies(one_ref, two_ref, out_ref):
    for i in range(HALF):
        out_ref[i, :RANK, :] = one_ref[...]
        out_ref[i, RANK:, :] = two_ref[...]


def side_by_side(in_ref):
    return jnp.concatenate([in_ref[i] for i in range(HALF)], axis=1)


def half_product(core_ref, own_ref, other_ref, both_ref, out_ref):
    core, both = core_ref[0], side_by_side(both_ref)
    out_ref[core] = lax.dot_general(side_by_side(own_ref), both, NT, preferred_element_type=F32)
    out_ref[1 - core] = lax.dot_general(side_by_side(other_ref), both, NT, preferred_element_type=F32)


def factors_of(parts_ref, out_ref):
    total = [(parts_ref[0, slot] + parts_ref[1, slot]).T for slot in range(2)]
    raw = [both[:RANK] for both in total]
    gram = [lax.dot_general(a, a, NT, precision=HIGH, preferred_element_type=F32) for a in raw]
    inverse = [inverse_cholesky(a) for a in gram]
    warm = [lax.dot_general(both[:RANK], both[RANK:], NT, precision=HIGH, preferred_element_type=F32) for both in total]
    for slot in range(2):
        both = jnp.concatenate([raw[slot], jnp.zeros((RANK, 192 - ROWS), F32), warm[slot]], axis=1)
        out_ref[slot] = jnp.dot(inverse[slot], both, precision=HIGH, preferred_element_type=F32).astype(BF16)


def against(core_ref, own_ref, other_ref, factors_ref, out_ref):
    core = core_ref[0]
    own, other = factors_ref[core, :, :ROWS], factors_ref[1 - core, :, :ROWS]
    at, to = pl.multiple_of(core * RANK, RANK), pl.multiple_of((1 - core) * RANK, RANK)
    for i in range(HALF):
        out_ref[i, pl.ds(at, RANK), :] = jnp.dot(
            own, own_ref[i], preferred_element_type=F32
        ).astype(BF16)
        out_ref[i, pl.ds(to, RANK), :] = jnp.dot(other, other_ref[i], preferred_element_type=F32).astype(BF16)


def project(core_ref, own_ref, other_ref, factors_ref, out_ref, term_ref):
    against(core_ref, own_ref, other_ref, factors_ref, out_ref)
    inner = jnp.concatenate([factors_ref[0, :, 192:], factors_ref[1, :, 192:]], axis=0)
    for i in range(HALF):
        term_ref[i] = lax.dot_general(inner, out_ref[i], TN, preferred_element_type=F32).astype(BF16)


def residual(core_ref, micro_ref, factors_ref, error_ref, right_ref):
    left = factors_ref[core_ref[0], :, :ROWS]
    upright = left.astype(F32).T.astype(BF16)
    strips = [slice(j * SLICE, (j + 1) * SLICE) for j in range(DP)]
    for at in strips:
        right_ref[:, at] = jnp.dot(left, micro_ref[:, at], preferred_element_type=F32).astype(BF16)
    for at in strips:
        approx = jnp.dot(upright, right_ref[:, at], preferred_element_type=F32)
        error_ref[:, at] = (micro_ref[:, at].astype(F32) - approx).astype(BF16)


def add_up(in_ref, out_ref):
    total = in_ref[0].astype(F32)
    for i in range(1, HALF):
        total += in_ref[i].astype(F32)
    out_ref[...] = total.astype(BF16)


def add_and_copy(in_ref, out_ref):
    total = in_ref[0].astype(F32)
    for i in range(1, HALF):
        total += in_ref[i].astype(F32)
    for i in range(HALF):
        out_ref[i] = total.astype(BF16)


def meet(whole_ref, terms_ref, out_ref):
    whole = side_by_side(whole_ref)
    out_ref[:, : 2 * RANK] = lax.dot_general(whole, side_by_side(terms_ref), NT, preferred_element_type=F32)
    out_ref[:, 2 * RANK : 3 * RANK] = lax.dot_general(whole, whole, NT, preferred_element_type=F32)
    out_ref[:, 3 * RANK :] = jnp.zeros((RANK, RANK), F32)


def add_met(parts_ref, out_ref):
    out_ref[...] = (parts_ref[0, :, : 2 * RANK] + parts_ref[1, :, : 2 * RANK]).astype(BF16)


def factor(parts_ref, out_ref):
    at = slice(2 * RANK, 3 * RANK)
    out_ref[...] = inverse_cholesky(parts_ref[0, :, at] + parts_ref[1, :, at])


def expand(met_ref, right_ref, out_ref):
    met = met_ref[...]
    for i in range(HALF):
        out_ref[i] = jnp.dot(met, right_ref[i], preferred_element_type=F32).astype(BF16)


def finish(inverse_ref, in_ref, out_ref):
    out_ref[...] = jnp.dot(inverse_ref[...], in_ref[...].astype(F32), precision=HIGH, preferred_element_type=F32)


LONG = 2**36
VMEM = pl.BlockSpec(memory_space=pltpu.VMEM)
SMEM = pl.BlockSpec(memory_space=pltpu.SMEM)


def kernel(body, *shapes, flops=0, moved=2**20, scratch=()):
    outs = [jax.ShapeDtypeStruct(shape, dtype) for shape, dtype in shapes]
    names = body.__code__.co_varnames[: body.__code__.co_argcount - len(outs) - len(scratch)]
    return pl.pallas_call(
        body,
        out_shape=outs if len(outs) > 1 else outs[0],
        in_specs=[SMEM if name == "core_ref" else VMEM for name in names],
        compiler_params=pltpu.CompilerParams(vmem_limit_bytes=10 * 2**20),
        cost_estimate=pl.CostEstimate(flops=flops, bytes_accessed=moved, transcendentals=0),
        scratch_shapes=list(scratch),
        name=body.__name__,
    )


def local(corrected, inputs, act_basis, weight_basis):
    micro, rows = corrected[0], inputs[0]
    core = (lax.axis_index("dp") % 2).reshape(1)
    product = 2 * ROWS * D * RANK
    halves = ((HALF, ROWS, SLICE), BF16)
    stacked = ((HALF, 2 * RANK, SLICE), BF16)
    blocks = ((HALF, RANK, SLICE), BF16)

    warm = passed_along(weight_basis[0].T, 1)
    micro_own, micro_other = kernel(split_halves, halves, halves)(core, micro)
    micro_other = exchanged(micro_other)
    both = kernel(copies, stacked, flops=LONG)(act_basis[0].T, warm)
    both, micro_other = lax.optimization_barrier((both, micro_other))
    both = across(both)
    part = kernel(half_product, ((2, ROWS, 2 * RANK), F32), flops=2 * product)(core, micro_own, micro_other, both)
    factors = kernel(factors_of, ((2, RANK, 256), BF16), flops=4 * product)(both_cores(part))
    factors_in = passed_along(factors, -1)
    rows_own, rows_other = kernel(split_halves, halves, halves)(core, lax.optimization_barrier((rows, factors))[0])
    rows_other = exchanged(rows_other)
    right = kernel(against, stacked, flops=LONG)(core, micro_own, micro_other, factors)
    error = kernel(residual, ((ROWS, D), BF16), flops=2 * product, scratch=[pltpu.VMEM((RANK, D), BF16)])(
        core, micro, factors
    )
    factors_in, rows_other, right = lax.optimization_barrier((factors_in, rows_other, right))
    terms, summed = kernel(project, stacked, blocks, flops=product)(core, rows_own, rows_other, factors_in)
    whole = across(kernel(add_and_copy, blocks)(across(summed)))
    met = both_cores(kernel(meet, ((RANK, 256), F32), flops=product)(whole, terms))
    met_in = passed_along(kernel(add_met, ((RANK, 2 * RANK), BF16))(met), 1)
    met_in, error = lax.optimization_barrier((met_in, error))
    parts = across(kernel(expand, blocks, flops=product)(met_in, right))
    parts = passed_along(kernel(add_up, ((RANK, SLICE), BF16))(parts), -1)
    inverse = kernel(factor, ((RANK, RANK), F32), flops=4 * product)(met)
    weight_right = kernel(finish, ((RANK, SLICE), F32))(inverse, parts)
    return error[None], weight_right.T[None]


def solution(mesh):
    spec = P("pipe", "dp", None)
    return jax.shard_map(local, mesh=mesh, in_specs=(spec,) * 4, out_specs=(spec, spec), check_vma=False)
```

```python
import functools

import jax
import jax.numpy as jnp
from jax import lax
from jax.experimental import pallas as pl
from jax.experimental.pallas import tpu as pltpu
from jax.sharding import PartitionSpec as P

HIGH = lax.Precision.HIGHEST
F32, BF16 = jnp.float32, jnp.bfloat16
D, RANK, ROWS, DP = 6144, 64, 136, 16
SLICE = D // DP
HALF = DP // 2
CORES = [[2 * i, 2 * i + 1] for i in range(HALF)]
ACROSS = [[2 * i + c for i in range(HALF)] for c in range(2)]
NT = (((1,), (1,)), ((), ()))
TN = (((0,), (0,)), ((), ()))


def passed_along(shard, by):
    devices = lax.axis_size("pipe")
    return lax.ppermute(shard, "pipe", [(i, (i + by) % devices) for i in range(devices)])


def exchanged(shard):
    return lax.ppermute(shard, "dp", [(i, i ^ 1) for i in range(DP)])


def both_cores(shard):
    return lax.all_gather(shard, "dp", axis_index_groups=CORES)


def across(blocks):
    return lax.all_to_all(blocks, "dp", 0, 0, tiled=True, axis_index_groups=ACROSS)


def strip(i, core):
    return pl.ds(pl.multiple_of((2 * i + core) * SLICE, 128), SLICE)


def inverse_cholesky(gram):
    wide = jnp.concatenate([gram, jnp.eye(RANK, dtype=F32)], axis=1)
    sub = lax.broadcasted_iota(jnp.int32, (8, 128), 0)
    part = [wide[8 * g : 8 * g + 8] for g in range(8)]
    for k in range(0, RANK, 4):
        own, r = divmod(k, 8)
        rows = [part[own][r + i : r + i + 1, :] for i in range(4)]
        s = {(i, j): jnp.broadcast_to(rows[i][:, k + j : k + j + 1], (1, 128)) for i in range(4) for j in range(i, 4)}
        a, b, c = s[0, 0], s[0, 1], s[1, 1]
        first = 1.0 / (a * c - b * b)
        e = [[(c * s[0, t] - b * s[1, t]) * first, (a * s[1, t] - b * s[0, t]) * first] for t in (2, 3)]
        d = s[2, 2] - s[0, 2] * e[0][0] - s[1, 2] * e[0][1]
        f = s[2, 3] - s[0, 2] * e[1][0] - s[1, 2] * e[1][1]
        h = s[3, 3] - s[0, 3] * e[1][0] - s[1, 3] * e[1][1]
        second = 1.0 / (d * h - f * f)
        y = [rows[2 + t] - e[t][0] * rows[0] - e[t][1] * rows[1] for t in (0, 1)]
        v = [(h * y[0] - f * y[1]) * second, (d * y[1] - f * y[0]) * second]
        z = [(c * rows[0] - b * rows[1]) * first, (a * rows[1] - b * rows[0]) * first]
        solved = [z[t] - e[0][t] * v[0] - e[1][t] * v[1] for t in (0, 1)] + v
        done = [rows[0], rows[1] - (b / a) * rows[0], y[0], y[1] - (f / d) * y[0]]
        for g in range(own, 8):
            if g > own or r == 0:
                less = part[g] - sum(part[g][:, k + i : k + i + 1] * solved[i] for i in range(4))
            if g > own:
                part[g] = less
            else:
                part[g] = jnp.where(sub > r + 3, less, part[g]) if r == 0 else part[g]
                for i in range(1, 4):
                    part[g] = jnp.where(sub == r + i, done[i], part[g])
    wide = jnp.concatenate(part, axis=0)
    square = (RANK, RANK)
    on_diagonal = lax.broadcasted_iota(jnp.int32, square, 0) == lax.broadcasted_iota(jnp.int32, square, 1)
    pivots = jnp.sum(jnp.where(on_diagonal, wide[:, :RANK], 0.0), axis=1, keepdims=True)
    return wide[:, RANK:] * lax.rsqrt(pivots)


def split_halves(core_ref, in_ref, own_ref, other_ref):
    core = core_ref[0]
    for i in range(HALF):
        own_ref[i] = in_ref[:, strip(i, core)]
        other_ref[i] = in_ref[:, strip(i, 1 - core)]


def copies(one_ref, two_ref, out_ref):
    for i in range(HALF):
        out_ref[i, :RANK, :] = one_ref[...]
        out_ref[i, RANK:, :] = two_ref[...]


def side_by_side(in_ref):
    return jnp.concatenate([in_ref[i] for i in range(HALF)], axis=1)


def half_product(core_ref, own_ref, other_ref, both_ref, out_ref):
    core, both = core_ref[0], side_by_side(both_ref)
    out_ref[core] = lax.dot_general(side_by_side(own_ref), both, NT, preferred_element_type=F32)
    out_ref[1 - core] = lax.dot_general(side_by_side(other_ref), both, NT, preferred_element_type=F32)


def factors_of(parts_ref, out_ref):
    total = [(parts_ref[0, slot] + parts_ref[1, slot]).T for slot in range(2)]
    raw = [both[:RANK] for both in total]
    gram = [lax.dot_general(a, a, NT, precision=HIGH, preferred_element_type=F32) for a in raw]
    inverse = [inverse_cholesky(a) for a in gram]
    warm = [lax.dot_general(both[:RANK], both[RANK:], NT, precision=HIGH, preferred_element_type=F32) for both in total]
    for slot in range(2):
        both = jnp.concatenate([raw[slot], jnp.zeros((RANK, 192 - ROWS), F32), warm[slot]], axis=1)
        out_ref[slot] = jnp.dot(inverse[slot], both, precision=HIGH, preferred_element_type=F32).astype(BF16)


def against(core_ref, own_ref, other_ref, factors_ref, out_ref):
    core = core_ref[0]
    own, other = factors_ref[core, :, :ROWS], factors_ref[1 - core, :, :ROWS]
    at, to = pl.multiple_of(core * RANK, RANK), pl.multiple_of((1 - core) * RANK, RANK)
    for i in range(HALF):
        out_ref[i, pl.ds(at, RANK), :] = jnp.dot(
            own, own_ref[i], preferred_element_type=F32
        ).astype(BF16)
        out_ref[i, pl.ds(to, RANK), :] = jnp.dot(other, other_ref[i], preferred_element_type=F32).astype(BF16)


def project(core_ref, own_ref, other_ref, factors_ref, out_ref, term_ref):
    against(core_ref, own_ref, other_ref, factors_ref, out_ref)
    inner = jnp.concatenate([factors_ref[0, :, 192:], factors_ref[1, :, 192:]], axis=0)
    for i in range(HALF):
        term_ref[i] = lax.dot_general(inner, out_ref[i], TN, preferred_element_type=F32).astype(BF16)


def residual(first, core_ref, micro_ref, factors_ref, *refs):
    error_ref, part_ref, sem = refs[-3:]
    left = factors_ref[core_ref[0], :, :ROWS]
    upright = left.astype(F32).T.astype(BF16)
    strips = [slice(j * SLICE, (j + 1) * SLICE) for j in range(HALF)]
    micro = [micro_ref[:, first + j * SLICE : first + (j + 1) * SLICE] for j in range(HALF)]
    right = [jnp.dot(left, part, preferred_element_type=F32).astype(BF16) for part in micro]
    for at, rows, part in zip(strips, micro, right):
        approx = jnp.dot(upright, part, preferred_element_type=F32)
        part_ref[:, at] = (rows.astype(F32) - approx).astype(BF16)
    move = pltpu.make_async_copy(part_ref, error_ref.at[:, first : first + D // 2], sem)
    move.start()
    move.wait()


def add_up(in_ref, out_ref):
    total = in_ref[0].astype(F32)
    for i in range(1, HALF):
        total += in_ref[i].astype(F32)
    out_ref[...] = total.astype(BF16)


def add_and_copy(in_ref, out_ref):
    total = in_ref[0].astype(F32)
    for i in range(1, HALF):
        total += in_ref[i].astype(F32)
    for i in range(HALF):
        out_ref[i] = total.astype(BF16)


def meet(whole_ref, terms_ref, out_ref):
    whole = side_by_side(whole_ref)
    out_ref[:, : 2 * RANK] = lax.dot_general(whole, side_by_side(terms_ref), NT, preferred_element_type=F32)
    out_ref[:, 2 * RANK : 3 * RANK] = lax.dot_general(whole, whole, NT, preferred_element_type=F32)
    out_ref[:, 3 * RANK :] = jnp.zeros((RANK, RANK), F32)


def add_met(parts_ref, out_ref):
    out_ref[...] = (parts_ref[0, :, : 2 * RANK] + parts_ref[1, :, : 2 * RANK]).astype(BF16)


def factor(parts_ref, out_ref):
    at = slice(2 * RANK, 3 * RANK)
    out_ref[...] = inverse_cholesky(parts_ref[0, :, at] + parts_ref[1, :, at])


def expand(met_ref, right_ref, out_ref):
    met = met_ref[...]
    for i in range(HALF):
        out_ref[i] = jnp.dot(met, right_ref[i], preferred_element_type=F32).astype(BF16)


def finish(inverse_ref, in_ref, out_ref):
    out_ref[...] = jnp.dot(inverse_ref[...], in_ref[...].astype(F32), precision=HIGH, preferred_element_type=F32)


LONG = 2**36
VMEM = pl.BlockSpec(memory_space=pltpu.VMEM)
ANY = pl.BlockSpec(memory_space=pl.ANY)
SMEM = pl.BlockSpec(memory_space=pltpu.SMEM)


def kernel(body, *shapes, flops=0, moved=2**20, scratch=()):
    outs = [jax.ShapeDtypeStruct(shape, dtype) for shape, dtype in shapes]
    names = body.__code__.co_varnames[: body.__code__.co_argcount - len(outs) - len(scratch)]
    return pl.pallas_call(
        body,
        out_shape=outs if len(outs) > 1 else outs[0],
        in_specs=[SMEM if name == "core_ref" else VMEM for name in names],
        compiler_params=pltpu.CompilerParams(vmem_limit_bytes=10 * 2**20),
        cost_estimate=pl.CostEstimate(flops=flops, bytes_accessed=moved, transcendentals=0),
        scratch_shapes=list(scratch),
        name=body.__name__,
    )


def remainder(first, core, micro, factors, *before):
    return pl.pallas_call(
        functools.partial(residual, first),
        out_shape=jax.ShapeDtypeStruct((ROWS, D), BF16),
        in_specs=[SMEM, VMEM, VMEM] + [ANY] * len(before),
        out_specs=ANY,
        scratch_shapes=[pltpu.VMEM((ROWS, D // 2), BF16), pltpu.SemaphoreType.DMA],
        input_output_aliases={3: 0} if before else {},
        compiler_params=pltpu.CompilerParams(vmem_limit_bytes=10 * 2**20),
        cost_estimate=pl.CostEstimate(flops=2 * ROWS * D * RANK, bytes_accessed=2**20, transcendentals=0),
        name="residual",
    )(core, micro, factors, *before)


def local(corrected, inputs, act_basis, weight_basis):
    micro, rows = corrected[0], inputs[0]
    core = (lax.axis_index("dp") % 2).reshape(1)
    product = 2 * ROWS * D * RANK
    halves = ((HALF, ROWS, SLICE), BF16)
    stacked = ((HALF, 2 * RANK, SLICE), BF16)
    blocks = ((HALF, RANK, SLICE), BF16)

    warm = passed_along(weight_basis[0].T, 1)
    micro_own, micro_other = kernel(split_halves, halves, halves)(core, micro)
    micro_other = exchanged(micro_other)
    rows_own, rows_other = kernel(split_halves, halves, halves)(core, rows)
    rows_other = exchanged(rows_other)
    both = kernel(copies, stacked, flops=LONG)(act_basis[0].T, warm)
    both, micro_other = lax.optimization_barrier((both, micro_other))
    both, rows_other = lax.optimization_barrier((across(both), rows_other))
    part = kernel(half_product, ((2, ROWS, 2 * RANK), F32), flops=2 * product)(core, micro_own, micro_other, both)
    factors = kernel(factors_of, ((2, RANK, 256), BF16), flops=4 * product)(both_cores(part))
    factors_in = passed_along(factors, -1)
    right = kernel(against, stacked, flops=product)(core, micro_own, micro_other, factors)
    error = remainder(0, core, micro, factors)
    factors_in, rows_other, right, error = lax.optimization_barrier((factors_in, rows_other, right, error))
    terms, summed = kernel(project, stacked, blocks, flops=product)(core, rows_own, rows_other, factors_in)
    whole = across(kernel(add_and_copy, blocks)(across(summed)))
    met = both_cores(kernel(meet, ((RANK, 256), F32), flops=product)(whole, terms))
    met_in = passed_along(kernel(add_met, ((RANK, 2 * RANK), BF16))(met), 1)
    met, error = lax.optimization_barrier((met, error))
    error = remainder(D // 2, core, micro, factors, error)
    met_in, error = lax.optimization_barrier((met_in, error))
    parts = across(kernel(expand, blocks, flops=product)(met_in, right))
    parts = passed_along(kernel(add_up, ((RANK, SLICE), BF16))(parts), -1)
    inverse = kernel(factor, ((RANK, RANK), F32), flops=4 * product)(met)
    weight_right = kernel(finish, ((RANK, SLICE), F32))(inverse, parts)
    return error[None], weight_right.T[None]


def solution(mesh):
    spec = P("pipe", "dp", None)
    return jax.shard_map(local, mesh=mesh, in_specs=(spec,) * 4, out_specs=(spec, spec), check_vma=False)
```

```python
import functools

import jax
import jax.numpy as jnp
from jax import lax
from jax.experimental import pallas as pl
from jax.experimental.pallas import tpu as pltpu
from jax.sharding import PartitionSpec as P

HIGH = lax.Precision.HIGHEST
F32, BF16 = jnp.float32, jnp.bfloat16
D, RANK, ROWS, DP = 6144, 64, 136, 16
SLICE = D // DP
HALF = DP // 2
CORES = [[2 * i, 2 * i + 1] for i in range(HALF)]
ACROSS = [[2 * i + c for i in range(HALF)] for c in range(2)]
NT = (((1,), (1,)), ((), ()))
TN = (((0,), (0,)), ((), ()))


def passed_along(shard, by):
    devices = lax.axis_size("pipe")
    return lax.ppermute(shard, "pipe", [(i, (i + by) % devices) for i in range(devices)])


def exchanged(shard):
    return lax.ppermute(shard, "dp", [(i, i ^ 1) for i in range(DP)])


def both_cores(shard):
    return lax.all_gather(shard, "dp", axis_index_groups=CORES)


def across(blocks):
    return lax.all_to_all(blocks, "dp", 0, 0, tiled=True, axis_index_groups=ACROSS)


def strip(i, core):
    return pl.ds(pl.multiple_of((2 * i + core) * SLICE, 128), SLICE)


def inverse_cholesky(gram):
    wide = jnp.concatenate([gram, jnp.eye(RANK, dtype=F32)], axis=1)
    sub = lax.broadcasted_iota(jnp.int32, (8, 128), 0)
    part = [wide[8 * g : 8 * g + 8] for g in range(8)]
    for k in range(0, RANK, 4):
        own, r = divmod(k, 8)
        rows = [part[own][r + i : r + i + 1, :] for i in range(4)]
        s = {(i, j): jnp.broadcast_to(rows[i][:, k + j : k + j + 1], (1, 128)) for i in range(4) for j in range(i, 4)}
        a, b, c = s[0, 0], s[0, 1], s[1, 1]
        first = 1.0 / (a * c - b * b)
        e = [[(c * s[0, t] - b * s[1, t]) * first, (a * s[1, t] - b * s[0, t]) * first] for t in (2, 3)]
        d = s[2, 2] - s[0, 2] * e[0][0] - s[1, 2] * e[0][1]
        f = s[2, 3] - s[0, 2] * e[1][0] - s[1, 2] * e[1][1]
        h = s[3, 3] - s[0, 3] * e[1][0] - s[1, 3] * e[1][1]
        second = 1.0 / (d * h - f * f)
        y = [rows[2 + t] - e[t][0] * rows[0] - e[t][1] * rows[1] for t in (0, 1)]
        v = [(h * y[0] - f * y[1]) * second, (d * y[1] - f * y[0]) * second]
        z = [(c * rows[0] - b * rows[1]) * first, (a * rows[1] - b * rows[0]) * first]
        solved = [z[t] - e[0][t] * v[0] - e[1][t] * v[1] for t in (0, 1)] + v
        done = [rows[0], rows[1] - (b / a) * rows[0], y[0], y[1] - (f / d) * y[0]]
        for g in range(own, 8):
            if g > own or r == 0:
                less = part[g] - sum(part[g][:, k + i : k + i + 1] * solved[i] for i in range(4))
            if g > own:
                part[g] = less
            else:
                part[g] = jnp.where(sub > r + 3, less, part[g]) if r == 0 else part[g]
                for i in range(1, 4):
                    part[g] = jnp.where(sub == r + i, done[i], part[g])
    wide = jnp.concatenate(part, axis=0)
    square = (RANK, RANK)
    on_diagonal = lax.broadcasted_iota(jnp.int32, square, 0) == lax.broadcasted_iota(jnp.int32, square, 1)
    pivots = jnp.sum(jnp.where(on_diagonal, wide[:, :RANK], 0.0), axis=1, keepdims=True)
    return wide[:, RANK:] * lax.rsqrt(pivots)


def split_halves(core_ref, in_ref, own_ref, other_ref):
    core = core_ref[0]
    for i in range(HALF):
        own_ref[i] = in_ref[:, strip(i, core)]
        other_ref[i] = in_ref[:, strip(i, 1 - core)]


def copies(one_ref, two_ref, out_ref):
    for i in range(HALF):
        out_ref[i, :RANK, :] = one_ref[...]
        out_ref[i, RANK:, :] = two_ref[...]


def side_by_side(in_ref):
    return jnp.concatenate([in_ref[i] for i in range(HALF)], axis=1)


def half_product(core_ref, own_ref, other_ref, both_ref, out_ref):
    core, both = core_ref[0], side_by_side(both_ref)
    out_ref[core] = lax.dot_general(side_by_side(own_ref), both, NT, preferred_element_type=F32)
    out_ref[1 - core] = lax.dot_general(side_by_side(other_ref), both, NT, preferred_element_type=F32)


def factors_of(parts_ref, out_ref):
    total = [(parts_ref[0, slot] + parts_ref[1, slot]).T for slot in range(2)]
    raw = [both[:RANK] for both in total]
    gram = [lax.dot_general(a, a, NT, precision=HIGH, preferred_element_type=F32) for a in raw]
    inverse = [inverse_cholesky(a) for a in gram]
    warm = [lax.dot_general(both[:RANK], both[RANK:], NT, precision=HIGH, preferred_element_type=F32) for both in total]
    wide = []
    for slot in range(2):
        both = jnp.concatenate([raw[slot], jnp.zeros((RANK, 192 - ROWS), F32), warm[slot]], axis=1)
        wide.append(jnp.dot(inverse[slot], both, precision=HIGH, preferred_element_type=F32))
    wide = jnp.concatenate(wide, axis=0)
    rest = wide[:, 128:].T
    out_ref[:128] = wide[:, :128].astype(BF16)
    out_ref[128:192] = rest[RANK:].astype(BF16)
    out_ref[192:] = rest[:16].astype(BF16)


def left_of(factors_ref, core):
    last = factors_ref[192:].astype(F32).T[:, : ROWS - 128].astype(BF16)
    left = jnp.concatenate([factors_ref[:128], last], axis=1)
    return jnp.where(core == 0, left[:RANK], left[RANK:])


def against(core_ref, own_ref, other_ref, factors_ref, out_ref):
    core = core_ref[0]
    own, other = left_of(factors_ref, core), left_of(factors_ref, 1 - core)
    at, to = pl.multiple_of(core * RANK, RANK), pl.multiple_of((1 - core) * RANK, RANK)
    for i in range(HALF):
        out_ref[i, pl.ds(at, RANK), :] = jnp.dot(
            own, own_ref[i], preferred_element_type=F32
        ).astype(BF16)
        out_ref[i, pl.ds(to, RANK), :] = jnp.dot(other, other_ref[i], preferred_element_type=F32).astype(BF16)


def project(core_ref, own_ref, other_ref, factors_ref, out_ref, term_ref):
    against(core_ref, own_ref, other_ref, factors_ref, out_ref)
    for i in range(HALF):
        term_ref[i] = jnp.dot(factors_ref[128:192], out_ref[i], preferred_element_type=F32).astype(BF16)


def residual(first, core_ref, micro_ref, factors_ref, *refs):
    error_ref, part_ref, sem = refs[-3:]
    left = left_of(factors_ref, core_ref[0])
    upright = left.astype(F32).T.astype(BF16)
    strips = [slice(j * SLICE, (j + 1) * SLICE) for j in range(HALF)]
    micro = [micro_ref[:, first + j * SLICE : first + (j + 1) * SLICE] for j in range(HALF)]
    right = [jnp.dot(left, part, preferred_element_type=F32).astype(BF16) for part in micro]
    for at, rows, part in zip(strips, micro, right):
        approx = jnp.dot(upright, part, preferred_element_type=F32)
        part_ref[:, at] = (rows.astype(F32) - approx).astype(BF16)
    move = pltpu.make_async_copy(part_ref, error_ref.at[:, first : first + D // 2], sem)
    move.start()
    move.wait()


def add_up(in_ref, out_ref):
    total = in_ref[0].astype(F32)
    for i in range(1, HALF):
        total += in_ref[i].astype(F32)
    out_ref[...] = total.astype(BF16)


def add_and_copy(in_ref, out_ref):
    total = in_ref[0].astype(F32)
    for i in range(1, HALF):
        total += in_ref[i].astype(F32)
    for i in range(HALF):
        out_ref[i] = total.astype(BF16)


def meet(whole_ref, terms_ref, out_ref):
    whole = side_by_side(whole_ref)
    out_ref[:, : 2 * RANK] = lax.dot_general(whole, side_by_side(terms_ref), NT, preferred_element_type=F32)
    out_ref[:, 2 * RANK : 3 * RANK] = lax.dot_general(whole, whole, NT, preferred_element_type=F32)
    out_ref[:, 3 * RANK :] = jnp.zeros((RANK, RANK), F32)


def add_met(parts_ref, out_ref):
    out_ref[...] = (parts_ref[0, :, : 2 * RANK] + parts_ref[1, :, : 2 * RANK]).astype(BF16)


def factor(parts_ref, out_ref):
    at = slice(2 * RANK, 3 * RANK)
    out_ref[...] = inverse_cholesky(parts_ref[0, :, at] + parts_ref[1, :, at])


def expand(met_ref, right_ref, out_ref):
    met = met_ref[...]
    for i in range(HALF):
        out_ref[i] = jnp.dot(met, right_ref[i], preferred_element_type=F32).astype(BF16)


def finish(inverse_ref, in_ref, out_ref):
    out_ref[...] = jnp.dot(inverse_ref[...], in_ref[...].astype(F32), precision=HIGH, preferred_element_type=F32)


LONG = 2**36
VMEM = pl.BlockSpec(memory_space=pltpu.VMEM)
ANY = pl.BlockSpec(memory_space=pl.ANY)
SMEM = pl.BlockSpec(memory_space=pltpu.SMEM)


def kernel(body, *shapes, flops=0, moved=2**20, scratch=()):
    outs = [jax.ShapeDtypeStruct(shape, dtype) for shape, dtype in shapes]
    names = body.__code__.co_varnames[: body.__code__.co_argcount - len(outs) - len(scratch)]
    return pl.pallas_call(
        body,
        out_shape=outs if len(outs) > 1 else outs[0],
        in_specs=[SMEM if name == "core_ref" else VMEM for name in names],
        compiler_params=pltpu.CompilerParams(vmem_limit_bytes=10 * 2**20),
        cost_estimate=pl.CostEstimate(flops=flops, bytes_accessed=moved, transcendentals=0),
        scratch_shapes=list(scratch),
        name=body.__name__,
    )


def remainder(first, core, micro, factors, *before):
    return pl.pallas_call(
        functools.partial(residual, first),
        out_shape=jax.ShapeDtypeStruct((ROWS, D), BF16),
        in_specs=[SMEM, VMEM, VMEM] + [ANY] * len(before),
        out_specs=ANY,
        scratch_shapes=[pltpu.VMEM((ROWS, D // 2), BF16), pltpu.SemaphoreType.DMA],
        input_output_aliases={3: 0} if before else {},
        compiler_params=pltpu.CompilerParams(vmem_limit_bytes=10 * 2**20),
        cost_estimate=pl.CostEstimate(flops=2 * ROWS * D * RANK, bytes_accessed=2**20, transcendentals=0),
        name="residual",
    )(core, micro, factors, *before)


def local(corrected, inputs, act_basis, weight_basis):
    micro, rows = corrected[0], inputs[0]
    core = (lax.axis_index("dp") % 2).reshape(1)
    product = 2 * ROWS * D * RANK
    halves = ((HALF, ROWS, SLICE), BF16)
    stacked = ((HALF, 2 * RANK, SLICE), BF16)
    blocks = ((HALF, RANK, SLICE), BF16)

    warm = passed_along(weight_basis[0].T, 1)
    micro_own, micro_other = kernel(split_halves, halves, halves)(core, micro)
    micro_other = exchanged(micro_other)
    rows_own, rows_other = kernel(split_halves, halves, halves)(core, rows)
    rows_other = exchanged(rows_other)
    both = kernel(copies, stacked, flops=LONG)(act_basis[0].T, warm)
    both, micro_other = lax.optimization_barrier((both, micro_other))
    both, rows_other = lax.optimization_barrier((across(both), rows_other))
    part = kernel(half_product, ((2, ROWS, 2 * RANK), F32), flops=2 * product)(core, micro_own, micro_other, both)
    factors = kernel(factors_of, ((208, 128), BF16), flops=4 * product)(both_cores(part))
    factors_in = passed_along(factors, -1)
    right = kernel(against, stacked, flops=product)(core, micro_own, micro_other, factors)
    error = remainder(0, core, micro, factors)
    factors_in, rows_other, right, error = lax.optimization_barrier((factors_in, rows_other, right, error))
    terms, summed = kernel(project, stacked, blocks, flops=product)(core, rows_own, rows_other, factors_in)
    whole = across(kernel(add_and_copy, blocks)(across(summed)))
    met = both_cores(kernel(meet, ((RANK, 256), F32), flops=product)(whole, terms))
    met_in = passed_along(kernel(add_met, ((RANK, 2 * RANK), BF16))(met), 1)
    met, error = lax.optimization_barrier((met, error))
    error = remainder(D // 2, core, micro, factors, error)
    met_in, error = lax.optimization_barrier((met_in, error))
    parts = across(kernel(expand, blocks, flops=product)(met_in, right))
    parts = passed_along(kernel(add_up, ((RANK, SLICE), BF16))(parts), -1)
    inverse = kernel(factor, ((RANK, RANK), F32), flops=4 * product)(met)
    weight_right = kernel(finish, ((RANK, SLICE), F32))(inverse, parts)
    return error[None], weight_right.T[None]


def solution(mesh):
    spec = P("pipe", "dp", None)
    return jax.shard_map(local, mesh=mesh, in_specs=(spec,) * 4, out_specs=(spec, spec), check_vma=False)
```

```python
import functools

import jax
import jax.numpy as jnp
from jax import lax
from jax.experimental import pallas as pl
from jax.experimental.pallas import tpu as pltpu
from jax.sharding import PartitionSpec as P

HIGH = lax.Precision.HIGHEST
F32, BF16 = jnp.float32, jnp.bfloat16
D, RANK, ROWS, DP = 6144, 64, 136, 16
SLICE = D // DP
HALF = DP // 2
CORES = [[2 * i, 2 * i + 1] for i in range(HALF)]
ACROSS = [[2 * i + c for i in range(HALF)] for c in range(2)]
NT = (((1,), (1,)), ((), ()))
TN = (((0,), (0,)), ((), ()))


def passed_along(shard, by):
    devices = lax.axis_size("pipe")
    return lax.ppermute(shard, "pipe", [(i, (i + by) % devices) for i in range(devices)])


def exchanged(shard):
    return lax.ppermute(shard, "dp", [(i, i ^ 1) for i in range(DP)])


def both_cores(shard):
    return lax.all_gather(shard, "dp", axis_index_groups=CORES)


def across(blocks):
    return lax.all_to_all(blocks, "dp", 0, 0, tiled=True, axis_index_groups=ACROSS)


def strip(i, core):
    return pl.ds(pl.multiple_of((2 * i + core) * SLICE, 128), SLICE)


def inverse_cholesky(gram):
    wide = jnp.concatenate([gram, jnp.eye(RANK, dtype=F32)], axis=1)
    sub = lax.broadcasted_iota(jnp.int32, (8, 128), 0)
    part = [wide[8 * g : 8 * g + 8] for g in range(8)]
    for k in range(0, RANK, 4):
        own, r = divmod(k, 8)
        rows = [part[own][r + i : r + i + 1, :] for i in range(4)]
        s = {(i, j): jnp.broadcast_to(rows[i][:, k + j : k + j + 1], (1, 128)) for i in range(4) for j in range(i, 4)}
        a, b, c = s[0, 0], s[0, 1], s[1, 1]
        first = 1.0 / (a * c - b * b)
        e = [[(c * s[0, t] - b * s[1, t]) * first, (a * s[1, t] - b * s[0, t]) * first] for t in (2, 3)]
        d = s[2, 2] - s[0, 2] * e[0][0] - s[1, 2] * e[0][1]
        f = s[2, 3] - s[0, 2] * e[1][0] - s[1, 2] * e[1][1]
        h = s[3, 3] - s[0, 3] * e[1][0] - s[1, 3] * e[1][1]
        second = 1.0 / (d * h - f * f)
        y = [rows[2 + t] - e[t][0] * rows[0] - e[t][1] * rows[1] for t in (0, 1)]
        v = [(h * y[0] - f * y[1]) * second, (d * y[1] - f * y[0]) * second]
        z = [(c * rows[0] - b * rows[1]) * first, (a * rows[1] - b * rows[0]) * first]
        solved = [z[t] - e[0][t] * v[0] - e[1][t] * v[1] for t in (0, 1)] + v
        done = [rows[0], rows[1] - (b / a) * rows[0], y[0], y[1] - (f / d) * y[0]]
        for g in range(own, 8):
            if g > own or r == 0:
                less = part[g] - sum(part[g][:, k + i : k + i + 1] * solved[i] for i in range(4))
            if g > own:
                part[g] = less
            else:
                part[g] = jnp.where(sub > r + 3, less, part[g]) if r == 0 else part[g]
                for i in range(1, 4):
                    part[g] = jnp.where(sub == r + i, done[i], part[g])
    wide = jnp.concatenate(part, axis=0)
    square = (RANK, RANK)
    on_diagonal = lax.broadcasted_iota(jnp.int32, square, 0) == lax.broadcasted_iota(jnp.int32, square, 1)
    pivots = jnp.sum(jnp.where(on_diagonal, wide[:, :RANK], 0.0), axis=1, keepdims=True)
    return wide[:, RANK:] * lax.rsqrt(pivots)


def split_halves(core_ref, in_ref, own_ref, other_ref):
    core = core_ref[0]
    for i in range(HALF):
        own_ref[i] = in_ref[:, strip(i, core)]
        other_ref[i] = in_ref[:, strip(i, 1 - core)]


def copies(one_ref, two_ref, out_ref):
    for i in range(HALF):
        out_ref[i, :RANK, :] = one_ref[...]
        out_ref[i, RANK:, :] = two_ref[...]


def side_by_side(in_ref):
    return jnp.concatenate([in_ref[i] for i in range(HALF)], axis=1)


def half_product(core_ref, own_ref, other_ref, both_ref, out_ref):
    core, both = core_ref[0], side_by_side(both_ref)
    out_ref[core] = lax.dot_general(side_by_side(own_ref), both, NT, preferred_element_type=F32)
    out_ref[1 - core] = lax.dot_general(side_by_side(other_ref), both, NT, preferred_element_type=F32)


def factors_of(parts_ref, out_ref):
    total = [(parts_ref[0, slot] + parts_ref[1, slot]).T for slot in range(2)]
    raw = [both[:RANK] for both in total]
    gram = [lax.dot_general(a, a, NT, precision=HIGH, preferred_element_type=F32) for a in raw]
    inverse = [inverse_cholesky(a) for a in gram]
    warm = [lax.dot_general(both[:RANK], both[RANK:], NT, precision=HIGH, preferred_element_type=F32) for both in total]
    wide = []
    for slot in range(2):
        both = jnp.concatenate([raw[slot], jnp.zeros((RANK, 192 - ROWS), F32), warm[slot]], axis=1)
        wide.append(jnp.dot(inverse[slot], both, precision=HIGH, preferred_element_type=F32))
    wide = jnp.concatenate(wide, axis=0)
    rest = wide[:, 128:].T
    out_ref[:128] = wide[:, :128].astype(BF16)
    out_ref[128:192] = rest[RANK:].astype(BF16)
    out_ref[192:] = rest[:16].astype(BF16)


def left_of(factors_ref, core):
    last = factors_ref[192:].astype(F32).T[:, : ROWS - 128].astype(BF16)
    left = jnp.concatenate([factors_ref[:128], last], axis=1)
    return jnp.where(core == 0, left[:RANK], left[RANK:])


def against(core_ref, own_ref, other_ref, factors_ref, out_ref):
    core = core_ref[0]
    own, other = left_of(factors_ref, core), left_of(factors_ref, 1 - core)
    at, to = pl.multiple_of(core * RANK, RANK), pl.multiple_of((1 - core) * RANK, RANK)
    for i in range(HALF):
        out_ref[i, pl.ds(at, RANK), :] = jnp.dot(
            own, own_ref[i], preferred_element_type=F32
        ).astype(BF16)
        out_ref[i, pl.ds(to, RANK), :] = jnp.dot(other, other_ref[i], preferred_element_type=F32).astype(BF16)


def project(core_ref, own_ref, other_ref, factors_ref, out_ref, term_ref):
    against(core_ref, own_ref, other_ref, factors_ref, out_ref)
    for i in range(HALF):
        term_ref[i] = jnp.dot(factors_ref[128:192], out_ref[i], preferred_element_type=F32).astype(BF16)


def residual(first, core_ref, micro_ref, factors_ref, *refs):
    error_ref, part_ref, sem = refs[-3:]
    left = left_of(factors_ref, core_ref[0])
    upright = left.astype(F32).T.astype(BF16)
    strips = [slice(j * SLICE, (j + 1) * SLICE) for j in range(HALF)]
    micro = [micro_ref[:, first + j * SLICE : first + (j + 1) * SLICE] for j in range(HALF)]
    right = [jnp.dot(left, part, preferred_element_type=F32).astype(BF16) for part in micro]
    for at, rows, part in zip(strips, micro, right):
        approx = jnp.dot(upright, part, preferred_element_type=F32)
        part_ref[:, at] = (rows.astype(F32) - approx).astype(BF16)
    move = pltpu.make_async_copy(part_ref, error_ref.at[:, first : first + D // 2], sem)
    move.start()
    move.wait()


def add_up(in_ref, out_ref):
    total = in_ref[0].astype(F32)
    for i in range(1, HALF):
        total += in_ref[i].astype(F32)
    out_ref[...] = total.astype(BF16)


def add_and_copy(in_ref, out_ref):
    total = in_ref[0].astype(F32)
    for i in range(1, HALF):
        total += in_ref[i].astype(F32)
    for i in range(HALF):
        out_ref[i] = total.astype(BF16)


def meet(whole_ref, terms_ref, out_ref):
    whole = side_by_side(whole_ref)
    out_ref[:RANK] = lax.dot_general(whole, side_by_side(terms_ref), NT, preferred_element_type=F32)
    gram = lax.dot_general(whole, whole, NT, preferred_element_type=F32)
    out_ref[RANK:] = jnp.concatenate([gram[:32], gram[32:]], axis=1)


def add_met(parts_ref, out_ref):
    out_ref[...] = (parts_ref[0, :RANK] + parts_ref[1, :RANK]).astype(BF16)


def factor(parts_ref, out_ref):
    gram = parts_ref[0, RANK:] + parts_ref[1, RANK:]
    out_ref[...] = inverse_cholesky(jnp.concatenate([gram[:, :RANK], gram[:, RANK:]], axis=0))


def expand(met_ref, right_ref, out_ref):
    met = met_ref[...]
    for i in range(HALF):
        out_ref[i] = jnp.dot(met, right_ref[i], preferred_element_type=F32).astype(BF16)


def finish(inverse_ref, in_ref, out_ref):
    out_ref[...] = jnp.dot(inverse_ref[...], in_ref[...].astype(F32), precision=HIGH, preferred_element_type=F32)


LONG = 2**36
VMEM = pl.BlockSpec(memory_space=pltpu.VMEM)
ANY = pl.BlockSpec(memory_space=pl.ANY)
SMEM = pl.BlockSpec(memory_space=pltpu.SMEM)


def kernel(body, *shapes, flops=0, moved=2**20, scratch=()):
    outs = [jax.ShapeDtypeStruct(shape, dtype) for shape, dtype in shapes]
    names = body.__code__.co_varnames[: body.__code__.co_argcount - len(outs) - len(scratch)]
    return pl.pallas_call(
        body,
        out_shape=outs if len(outs) > 1 else outs[0],
        in_specs=[SMEM if name == "core_ref" else VMEM for name in names],
        compiler_params=pltpu.CompilerParams(vmem_limit_bytes=10 * 2**20),
        cost_estimate=pl.CostEstimate(flops=flops, bytes_accessed=moved, transcendentals=0),
        scratch_shapes=list(scratch),
        name=body.__name__,
    )


def remainder(first, core, micro, factors, *before):
    return pl.pallas_call(
        functools.partial(residual, first),
        out_shape=jax.ShapeDtypeStruct((ROWS, D), BF16),
        in_specs=[SMEM, VMEM, VMEM] + [ANY] * len(before),
        out_specs=ANY,
        scratch_shapes=[pltpu.VMEM((ROWS, D // 2), BF16), pltpu.SemaphoreType.DMA],
        input_output_aliases={3: 0} if before else {},
        compiler_params=pltpu.CompilerParams(vmem_limit_bytes=10 * 2**20),
        cost_estimate=pl.CostEstimate(flops=2 * ROWS * D * RANK, bytes_accessed=2**20, transcendentals=0),
        name="residual",
    )(core, micro, factors, *before)


def local(corrected, inputs, act_basis, weight_basis):
    micro, rows = corrected[0], inputs[0]
    core = (lax.axis_index("dp") % 2).reshape(1)
    product = 2 * ROWS * D * RANK
    halves = ((HALF, ROWS, SLICE), BF16)
    stacked = ((HALF, 2 * RANK, SLICE), BF16)
    blocks = ((HALF, RANK, SLICE), BF16)

    warm = passed_along(weight_basis[0].T, 1)
    micro_own, micro_other = kernel(split_halves, halves, halves)(core, micro)
    micro_other = exchanged(micro_other)
    rows_own, rows_other = kernel(split_halves, halves, halves)(core, rows)
    rows_other = exchanged(rows_other)
    both = kernel(copies, stacked, flops=LONG)(act_basis[0].T, warm)
    both, micro_other = lax.optimization_barrier((both, micro_other))
    both, rows_other = lax.optimization_barrier((across(both), rows_other))
    part = kernel(half_product, ((2, ROWS, 2 * RANK), F32), flops=2 * product)(core, micro_own, micro_other, both)
    factors = kernel(factors_of, ((208, 128), BF16), flops=4 * product)(both_cores(part))
    factors_in = passed_along(factors, -1)
    right = kernel(against, stacked, flops=product)(core, micro_own, micro_other, factors)
    error = remainder(0, core, micro, factors)
    factors_in, rows_other, right, error = lax.optimization_barrier((factors_in, rows_other, right, error))
    terms, summed = kernel(project, stacked, blocks, flops=product)(core, rows_own, rows_other, factors_in)
    whole = across(kernel(add_and_copy, blocks)(across(summed)))
    met = both_cores(kernel(meet, ((96, 2 * RANK), F32), flops=product)(whole, terms))
    met_in = passed_along(kernel(add_met, ((RANK, 2 * RANK), BF16))(met), 1)
    met, error = lax.optimization_barrier((met, error))
    error = remainder(D // 2, core, micro, factors, error)
    met_in, error = lax.optimization_barrier((met_in, error))
    parts = across(kernel(expand, blocks, flops=product)(met_in, right))
    parts = passed_along(kernel(add_up, ((RANK, SLICE), BF16))(parts), -1)
    inverse = kernel(factor, ((RANK, RANK), F32), flops=4 * product)(met)
    weight_right = kernel(finish, ((RANK, SLICE), F32))(inverse, parts)
    return error[None], weight_right.T[None]


def solution(mesh):
    spec = P("pipe", "dp", None)
    return jax.shard_map(local, mesh=mesh, in_specs=(spec,) * 4, out_specs=(spec, spec), check_vma=False)
```
